128 devices in a mesh: seq: 8 (over x, core), chan: 16 (over y, z).
Axes of the slice: x: 4, y: 4, z: 4, core: 2. Of those that a mesh axis runs over, the one named last changes fastest.
Arguments:
- query_proj: bfloat16 [16384, 8192], P('seq', 'chan'), may hold values from -6 to 6
- key_proj: bfloat16 [16384, 8192], P('seq', 'chan'), may hold values from -6 to 6
- value_proj: bfloat16 [16384, 8192], P('seq', 'chan'), may hold values from -6 to 6
- pole_rate: float32 [16, 8192], P(None, 'chan'), may hold values from 1.2207031e-05 to 0.0333333333
- pole_residue: float32 [16, 8192], P(None, 'chan'), may hold values from -0.3 to 0.3
- skip_gain: float32 [8192], P('chan'), may hold values from 0.5 to 1.5
- out_weight: bfloat16 [8192, 8192], P('chan'), may hold values from -0.0625 to 0.0625
Outputs:
- layer_out: bfloat16 [16384, 8192], P(('seq', 'chan'))
The draws below stay inside these ranges and needn't reach their ends.
All inputs are finite; a program needn't handle non-finite values.
Results may differ from the reference program's by a relative error of at most 0.02.
Values may be sent and summed in bfloat16 or wider, within the bound.
No kernel may reach another device: no remote copies, remote signals or barrier semaphores. Data moves between devices by JAX's collectives and lax.ppermute only.
A program may use at most 192 MiB of HBM per device.

```python
import jax
import jax.numpy as jnp
from jax import lax

D = 8192
POLES = 16
LENGTH = 16384
N_CHAN = 16


def pole_pair(key, slow_share):
    parts = jax.random.split(key, 4)
    slow = jax.random.bernoulli(parts[0], slow_share, (POLES, D))
    slow_rate = jnp.exp(jax.random.uniform(parts[1], (POLES, D), jnp.float32, jnp.log(0.2 / LENGTH), jnp.log(2.0 / LENGTH)))
    fast_rate = jnp.exp(jax.random.uniform(parts[2], (POLES, D), jnp.float32, jnp.log(1.0 / 50.0), jnp.log(1.0 / 30.0)))
    rates = jnp.where(slow, slow_rate, fast_rate)
    normal_part = jnp.clip(jax.random.normal(parts[3], (POLES, D), jnp.float32), -4.0, 4.0)
    residues = normal_part * jnp.sqrt(2.0 * rates / POLES)
    return (rates, residues)


def draw_pole_rate(key, part):
    share = 0.5
    rates, residues = pole_pair(key, share)
    return rates


def draw_pole_residue(key, part):
    share = 0.5
    rates, residues = pole_pair(key, share)
    return residues


def block_scale(rng, dims, cuts, low, largest):
    def one(dim, shards_of):
        steps = jax.random.uniform(jax.random.fold_in(jax.random.fold_in(rng, 6), dim), (shards_of,), jnp.float32, low / len(cuts), largest / len(cuts))
        return jnp.repeat(jnp.exp(steps), dims[dim] // shards_of).reshape((-1,) + (1,) * (len(dims) - dim - 1))

    level = one(*cuts[0])
    for cut in cuts[1:]:
        level = level * one(*cut)
    return level


def gaussian(rng, dims, scale, bound, cuts=(), kind=jnp.bfloat16):
    loudness = block_scale(rng, dims, cuts, -0.22, 0.18) if cuts else 1.0
    result = jax.random.normal(rng, dims, jnp.float32) * scale * loudness
    return jnp.minimum(jnp.maximum(result, -bound), bound).astype(kind)


def setup_inputs(seed: int = 0) -> dict:
    streams_of = jax.random.split(jax.random.key(seed), 8)
    return {
        "query_proj": gaussian(streams_of[0], (LENGTH, D), 1.0, 6.0, ((0, 8), (1, 16))),
        "key_proj": gaussian(streams_of[1], (LENGTH, D), 1.0, 6.0, ((0, 8), (1, 16))),
        "value_proj": gaussian(streams_of[2], (LENGTH, D), 1.0, 6.0, ((0, 8), (1, 16))),
        "pole_rate": draw_pole_rate(jax.random.fold_in(streams_of[7], 71), 0),
        "pole_residue": draw_pole_residue(jax.random.fold_in(streams_of[7], 71), 0),
        "skip_gain": jnp.clip(0.5 + 1.0 * jax.random.uniform(streams_of[5], (D,), jnp.float32) ** block_scale(streams_of[5], (D,), ((0, 16),), -0.2, 0.2), 0.5, 1.5),
        "out_weight": gaussian(streams_of[6], (D, D), D ** -0.5, 0.0625, ((0, 16),)),
    }


def reference(query_proj, key_proj, value_proj, pole_rate, pole_residue, skip_gain, out_weight):
    drive = key_proj.astype(jnp.float32) * value_proj.astype(jnp.float32)
    factor = jnp.exp(-pole_rate)

    def advance(state, row):
        state = factor * state + row[None, :]
        return state, jnp.sum(pole_residue * state, axis=0)

    _, conv = lax.scan(advance, jnp.zeros(pole_rate.shape, jnp.float32), drive)
    mixed = (query_proj.astype(jnp.float32) * (conv + skip_gain[None, :] * drive)).astype(jnp.bfloat16)
    group = D // N_CHAN
    mixed_groups = jnp.transpose(mixed.reshape(mixed.shape[0], N_CHAN, group), (1, 0, 2))
    weight_groups = out_weight.reshape(N_CHAN, group, out_weight.shape[1])

    def accumulate(total, pair):
        partial_value = jnp.dot(pair[0], pair[1], preferred_element_type=jnp.float32).astype(jnp.bfloat16)
        return total + partial_value.astype(jnp.float32), None

    total, _ = lax.scan(accumulate, jnp.zeros((mixed.shape[0], out_weight.shape[1]), jnp.float32),
                        (mixed_groups, weight_groups))
    return total.astype(jnp.bfloat16)
```

```python
import functools
import jax, jax.numpy as jnp
from jax import lax
from jax.experimental import pallas as pl
from jax.experimental.pallas import tpu as pltpu
from jax.sharding import PartitionSpec as P
POLES=16

def state_kernel(k_ref, v_ref, rate_ref, excl_ref, span_ref, drive, fb, *, T, unroll):
    W = k_ref.shape[-1]
    nO = k_ref.shape[0]
    drive[...] = (k_ref[...].astype(jnp.float32) * v_ref[...].astype(jnp.float32)).reshape(nO*T, W)
    rate = rate_ref[...]
    f = jnp.exp(-rate)
    for r in range(POLES):
        fb[r] = jnp.broadcast_to(f[r:r+1], (8, W))
    oid = lax.broadcasted_iota(jnp.int32, (8, W), 0)
    prev = None
    fT = jnp.exp(-rate * T)
    finals = []
    for p in range(nO//8):
        def body(i, s):
            s = list(s)
            for j in range(unroll):
                u = drive[pl.ds(p*8*T + i*unroll + j, 8, stride=T), :]
                for r in range(POLES):
                    s[r] = fb[r]*s[r] + u
            return tuple(s)
        s = lax.fori_loop(0, T//unroll, body, tuple(jnp.zeros((8,W),jnp.float32) for _ in range(POLES)))
        finals.append(s)
    spans=[]
    for r in range(POLES):
        carry = jnp.zeros((1,W),jnp.float32)
        g = fT[r:r+1]
        g2 = g*g; g4 = g2*g2; g8 = g4*g4
        pw = jnp.ones((8,W),jnp.float32)
        pw = jnp.where((oid & 1)!=0, pw*g, pw)
        pw = jnp.where((oid & 2)!=0, pw*g2, pw)
        pw = jnp.where((oid & 4)!=0, pw*g4, pw)
        for p in range(nO//8):
            s = finals[p][r]
            for d, gd in ((1,g),(2,g2),(4,g4)):
                s = s + jnp.where(oid>=d, pltpu.roll(s, d, 0), 0.0)*gd
            ex = jnp.where(oid>=1, pltpu.roll(s,1,0), 0.0) + pw*carry
            excl_ref[r, pl.ds(p*8,8), :] = ex
            carry = s[7:8] + g8*carry
        spans.append(carry)
    span_ref[...] = jnp.concatenate(spans, axis=0)

def states(k3, v3, rate, unroll=4):
    nO,T,C = k3.shape
    W=128
    return pl.pallas_call(
        functools.partial(state_kernel, T=T, unroll=unroll),
        grid=(C//W,),
        in_specs=[pl.BlockSpec((nO,T,W), lambda c:(0,0,c)), pl.BlockSpec((nO,T,W), lambda c:(0,0,c)),
                  pl.BlockSpec((POLES,W), lambda c:(0,c))],
        out_specs=[pl.BlockSpec((POLES,nO,W), lambda c:(0,0,c)), pl.BlockSpec((POLES,W), lambda c:(0,c))],
        out_shape=[jax.ShapeDtypeStruct((POLES,nO,C), jnp.float32), jax.ShapeDtypeStruct((POLES,C), jnp.float32)],
        scratch_shapes=[pltpu.VMEM((nO*T,W), jnp.float32), pltpu.VMEM((POLES,8,W), jnp.float32)],
        name="states",
    )(k3, v3, rate)

def conv_kernel(q_ref, k_ref, v_ref, rate_ref, res_ref, skip_ref, init_ref, out_ref, state_ref, drive, y, fb, rb, *, unroll):
    nO, T, W = k_ref.shape
    drive[...] = (k_ref[...].astype(jnp.float32) * v_ref[...].astype(jnp.float32)).reshape(nO*T, W)
    f = jnp.exp(-rate_ref[...])
    for r in range(POLES):
        fb[r] = jnp.broadcast_to(f[r:r+1], (8, W))
        rb[r] = jnp.broadcast_to(res_ref[r:r+1], (8, W))
    rb[POLES] = jnp.broadcast_to(skip_ref[...], (8, W))
    for p in range(nO//8):
        def body(i, s):
            s = list(s)
            for j in range(unroll):
                t = i*unroll + j
                u = drive[pl.ds(p*8*T + t, 8, stride=T), :]
                acc = [rb[POLES]*u, None, None, None]
                for r in range(POLES):
                    s[r] = fb[r]*s[r] + u
                    m = rb[r]*s[r]
                    acc[r%4] = m if acc[r%4] is None else acc[r%4] + m
                y[pl.ds(p*8*T + t, 8, stride=T), :] = (acc[0]+acc[1])+(acc[2]+acc[3])
            return tuple(s)
        s = lax.fori_loop(0, T//unroll, body, tuple(init_ref[r, pl.ds(p*8,8), :] for r in range(POLES)))
        for r in range(POLES):
            state_ref[r, pl.ds(p*8,8), :] = s[r]
    out_ref[...] = (q_ref[...].astype(jnp.float32) * y[...].reshape(nO,T,W)).astype(jnp.bfloat16)

def conv_chunk(q3,k3,v3,rate,res,skip,init,i,tc,unroll=4):
    nO,T,C = k3.shape
    W=128
    row = pl.BlockSpec((nO,tc,W), lambda c:(0,i,c))
    par = pl.BlockSpec((POLES,W), lambda c:(0,c))
    st = pl.BlockSpec((POLES,nO,W), lambda c:(0,0,c))
    return pl.pallas_call(
        functools.partial(conv_kernel, unroll=unroll),
        grid=(C//W,),
        in_specs=[row,row,row,par,par,pl.BlockSpec((1,W), lambda c:(0,c)),st],
        out_specs=[pl.BlockSpec((nO,tc,W), lambda c:(0,0,c)), st],
        out_shape=[jax.ShapeDtypeStruct((nO,tc,C), jnp.bfloat16), jax.ShapeDtypeStruct((POLES,nO,C), jnp.float32)],
        scratch_shapes=[pltpu.VMEM((nO*tc,W), jnp.float32), pltpu.VMEM((nO*tc,W), jnp.float32), pltpu.VMEM((POLES,8,W), jnp.float32), pltpu.VMEM((POLES+1,8,W), jnp.float32)],
        name="conv",
    )(q3,k3,v3,rate,res,skip.reshape(1,-1),init)


def incoming_state(span, rate, rows):
    devices = lax.axis_size("seq")
    me = lax.axis_index("seq")
    spans = lax.all_gather(span, "seq", axis=0)
    gap = (me - 1 - jnp.arange(devices)).astype(jnp.float32)[:, None, None]
    weight = jnp.where(gap >= 0, jnp.exp(-rate[None] * rows * jnp.maximum(gap, 0.0)), 0.0)
    return jnp.sum(weight * spans, axis=0)


def local(query_proj, key_proj, value_proj, pole_rate, pole_residue, skip_gain, out_weight):
    rows, width = key_proj.shape
    owners = lax.axis_size("chan")
    per = rows // owners
    q3, k3, v3 = [x.reshape(owners, per, width) for x in (query_proj, key_proj, value_proj)]
    excl, span = states(k3, v3, pole_rate)
    incoming = incoming_state(span, pole_rate, rows)
    index = jnp.arange(owners, dtype=jnp.float32)[None, :, None]
    init = excl + jnp.exp(-pole_rate[:, None, :] * per * index) * incoming[:, None, :]
    mixed, _ = conv_chunk(q3, k3, v3, pole_rate, pole_residue, skip_gain, init, 0, per)
    mixed = mixed.reshape(rows, width)
    parts = []
    chunks = 4
    cols = out_weight.shape[1] // chunks
    for j in range(chunks):
        weight = lax.slice_in_dim(out_weight, j * cols, (j + 1) * cols, axis=1)
        partial = jnp.dot(mixed, weight, preferred_element_type=jnp.float32).astype(jnp.bfloat16)
        parts.append(lax.psum_scatter(partial, "chan", scatter_dimension=0, tiled=True))
    return jnp.concatenate(parts, axis=1)


def solution(mesh):
    in_specs = (
        P("seq", "chan"),
        P("seq", "chan"),
        P("seq", "chan"),
        P(None, "chan"),
        P(None, "chan"),
        P("chan"),
        P("chan", None),
    )
    out_specs = P(("seq", "chan"), None)
    return jax.shard_map(local, mesh=mesh, in_specs=in_specs, out_specs=out_specs, check_vma=False)
```

```python
import functools

import jax
import jax.numpy as jnp
from jax import lax
from jax.experimental import pallas as pl
from jax.experimental.pallas import tpu as pltpu
from jax.sharding import PartitionSpec as P

POLES = 16
LANES = 128
NX, NCORE, NY, NZ = 4, 2, 4, 4
STEPS = (1, -1, 2)
ROW_PARTS = (2, 2, 4)
COL_PARTS = (2, 2, 4)
TILES = (((0,), (0,)), ((1,), (0,)), ((0, 1), (1,)), ((2,), (0, 1)), ((0, 1), (2,)), ((2,), (2,)))
ANY = pl.BlockSpec(memory_space=pl.ANY)
SMEM = pl.BlockSpec(memory_space=pltpu.SMEM)
VMEM = pl.BlockSpec(memory_space=pltpu.VMEM)
LIMIT = pltpu.CompilerParams(vmem_limit_bytes=48 * 1024 * 1024)


def over_y(value, step):
    return lax.ppermute(value, "chan", [(y * NZ + z, (y + step) % NY * NZ + z) for y in range(NY) for z in range(NZ)])


def over_z(value, step):
    return lax.ppermute(value, "chan", [(y * NZ + z, y * NZ + (z + step) % NZ) for y in range(NY) for z in range(NZ)])


def with_partner(value):
    return lax.ppermute(value, "chan", [(y * NZ + z, (y ^ 1) * NZ + z) for y in range(NY) for z in range(NZ)])


def other_core(value):
    return lax.ppermute(value, "seq", [(s, s ^ 1) for s in range(NX * NCORE)])


def from_chip_behind(value, step):
    pairs = [(x * NCORE + c, (x + step) * NCORE + c) for x in range(NX - step) for c in range(NCORE)]
    return lax.ppermute(value, "seq", pairs)


def state_kernel(k_ref, v_ref, rate_ref, excl_ref, span_ref, drive, fb, *, T, unroll):
    W = k_ref.shape[-1]
    nO = k_ref.shape[0]
    drive[...] = (k_ref[...].astype(jnp.float32) * v_ref[...].astype(jnp.float32)).reshape(nO*T, W)
    rate = rate_ref[...]
    f = jnp.exp(-rate)
    for r in range(POLES):
        fb[r] = jnp.broadcast_to(f[r:r+1], (8, W))
    oid = lax.broadcasted_iota(jnp.int32, (8, W), 0)
    prev = None
    fT = jnp.exp(-rate * T)
    finals = []
    G = nO//8
    fr = [fb[r] for r in range(POLES)]
    def body(i, s):
        s = [list(x) for x in s]
        for j in range(unroll):
            for p in range(G):
                u = drive[pl.ds(p*8*T + i*unroll + j, 8, stride=T), :]
                for r in range(POLES):
                    s[p][r] = fr[r]*s[p][r] + u
        return tuple(tuple(x) for x in s)
    finals = lax.fori_loop(0, T//unroll, body, tuple(tuple(jnp.zeros((8,W),jnp.float32) for _ in range(POLES)) for p in range(G)))
    spans=[]
    for r in range(POLES):
        carry = jnp.zeros((1,W),jnp.float32)
        g = fT[r:r+1]
        g2 = g*g; g4 = g2*g2; g8 = g4*g4
        pw = jnp.ones((8,W),jnp.float32)
        pw = jnp.where((oid & 1)!=0, pw*g, pw)
        pw = jnp.where((oid & 2)!=0, pw*g2, pw)
        pw = jnp.where((oid & 4)!=0, pw*g4, pw)
        for p in range(nO//8):
            s = finals[p][r]
            for d, gd in ((1,g),(2,g2),(4,g4)):
                s = s + jnp.where(oid>=d, pltpu.roll(s, d, 0), 0.0)*gd
            ex = jnp.where(oid>=1, pltpu.roll(s,1,0), 0.0) + pw*carry
            excl_ref[r, pl.ds(p*8,8), :] = ex
            carry = s[7:8] + g8*carry
        spans.append(carry)
    span_ref[...] = jnp.concatenate(spans, axis=0)

def states(k3, v3, rate, unroll=4):
    nO,T,C = k3.shape
    W=128
    return pl.pallas_call(
        functools.partial(state_kernel, T=T, unroll=unroll),
        grid=(C//W,),
        in_specs=[pl.BlockSpec((nO,T,W), lambda c:(0,0,c)), pl.BlockSpec((nO,T,W), lambda c:(0,0,c)),
                  pl.BlockSpec((POLES,W), lambda c:(0,c))],
        out_specs=[pl.BlockSpec((POLES,nO,W), lambda c:(0,0,c)), pl.BlockSpec((POLES,W), lambda c:(0,c))],
        out_shape=[jax.ShapeDtypeStruct((POLES,nO,C), jnp.float32), jax.ShapeDtypeStruct((POLES,C), jnp.float32)],
        scratch_shapes=[pltpu.VMEM((nO*T,W), jnp.float32), pltpu.VMEM((POLES,8,W), jnp.float32)],
        name="states",
    )(k3, v3, rate)


def conv_kernel(pos_ref, q_ref, k_ref, v_ref, rate_ref, res_ref, skip_ref, init_ref, *rest, unroll, per, first, last):
    rest = list(rest)
    inc_ref = rest.pop(0) if first else None
    outs = rest[:4]
    state_ref = None if last else rest[4]
    drive, y, fb, rb, mixed = rest[4 if last else 5:]
    nO, T, W = k_ref.shape
    drive[...] = (k_ref[...].astype(jnp.float32) * v_ref[...].astype(jnp.float32)).reshape(nO * T, W)
    rate = rate_ref[...]
    f = jnp.exp(-rate)
    for r in range(POLES):
        fb[r] = jnp.broadcast_to(f[r:r + 1], (8, W))
        rb[r] = jnp.broadcast_to(res_ref[r:r + 1], (8, W))
    rb[POLES] = jnp.broadcast_to(skip_ref[...], (8, W))
    fr = [fb[r] for r in range(POLES)]
    G = nO // 8

    def begin(p, r):
        s = init_ref[r, pl.ds(p * 8, 8), :]
        if first:
            owner = (lax.broadcasted_iota(jnp.int32, (8, W), 0) + p * 8).astype(jnp.float32)
            s = s + jnp.exp(-(rate[r:r + 1] * float(per)) * owner) * inc_ref[r:r + 1]
        return s

    def body(i, s):
        s = [list(x) for x in s]
        for j in range(unroll):
            t = i * unroll + j
            us = [drive[pl.ds(p * 8 * T + t, 8, stride=T), :] for p in range(G)]
            acc = [[rb[POLES] * us[p], None] for p in range(G)]
            for r in range(POLES):
                rr = rb[r]
                for p in range(G):
                    s[p][r] = fr[r] * s[p][r] + us[p]
                    m = rr * s[p][r]
                    acc[p][r % 2] = m if acc[p][r % 2] is None else acc[p][r % 2] + m
            for p in range(G):
                y[pl.ds(p * 8 * T + t, 8, stride=T), :] = acc[p][0] + acc[p][1]
        return tuple(tuple(x) for x in s)

    s = lax.fori_loop(0, T // unroll, body, tuple(tuple(begin(p, r) for r in range(POLES)) for p in range(G)))
    if not last:
        for p in range(G):
            for r in range(POLES):
                state_ref[r, pl.ds(p * 8, 8), :] = s[p][r]
    mixed[...] = (q_ref[...].astype(jnp.float32) * y[...].reshape(nO, T, W)).astype(jnp.bfloat16)
    my_y, my_z = pos_ref[0], pos_ref[1]
    for out_ref, step in zip(outs, (0,) + STEPS):
        half = lax.rem(my_y + step + NY, NY) // 2
        for zr in range(NZ):
            z = lax.rem(my_z + zr, NZ)
            for yl in range(2):
                out_ref[zr, yl] = mixed[half * 8 + yl * NZ + z]


def conv_chunk(pos, q3, k3, v3, rate, res, skip, init, inc, index, tc, last):
    nO, T, C = k3.shape
    W = LANES
    first = inc is not None
    row = pl.BlockSpec((nO, tc, W), lambda c: (0, index, c))
    par = pl.BlockSpec((POLES, W), lambda c: (0, c))
    st = pl.BlockSpec((POLES, nO, W), lambda c: (0, 0, c))
    ops = [pos, q3, k3, v3, rate, res, skip.reshape(1, -1), init]
    specs = [SMEM, row, row, row, par, par, pl.BlockSpec((1, W), lambda c: (0, c)), st]
    if first:
        ops.append(inc)
        specs.append(par)
    out = jax.ShapeDtypeStruct((NZ, 2, tc, C), jnp.bfloat16)
    out_shape = [out] * 4
    out_specs = [pl.BlockSpec((NZ, 2, tc, W), lambda c: (0, 0, 0, c))] * 4
    if not last:
        out_shape = out_shape + [jax.ShapeDtypeStruct((POLES, nO, C), jnp.float32)]
        out_specs = out_specs + [st]
    res = pl.pallas_call(
        functools.partial(conv_kernel, unroll=4, per=T, first=first, last=last),
        grid=(C // W,),
        in_specs=specs,
        out_specs=out_specs,
        out_shape=out_shape,
        scratch_shapes=[
            pltpu.VMEM((nO * tc, W), jnp.float32),
            pltpu.VMEM((nO * tc, W), jnp.float32),
            pltpu.VMEM((POLES, 8, W), jnp.float32),
            pltpu.VMEM((POLES + 1, 8, W), jnp.float32),
            pltpu.VMEM((nO, tc, W), jnp.bfloat16),
        ],
        compiler_params=LIMIT,
        cost_estimate=pl.CostEstimate(flops=nO * tc * C * POLES * 4, bytes_accessed=nO * tc * C * 10, transcendentals=0),
        name="conv",
    )(*ops)
    return res[:4], (None if last else res[4])


def share_kernel(pos_ref, w_ref, *refs, widths, offsets, half_cols):
    n = len(widths) * len(STEPS)
    outs, sems = refs[:n], refs[n]
    copies = []
    for g, (width, offset) in enumerate(zip(widths, offsets)):
        for i, step in enumerate(STEPS):
            half = lax.rem(lax.rem(pos_ref[0] + step + NY, NY), 2)
            col = pl.multiple_of(half * half_cols + offset + pos_ref[2] * width, LANES)
            k = g * len(STEPS) + i
            copies.append(pltpu.make_async_copy(w_ref.at[:, pl.ds(col, width)], outs[k], sems.at[k]))
    for c in copies:
        c.start()
    for c in copies:
        c.wait()


def weight_shares(pos, weight, widths, offsets, half_cols):
    k = weight.shape[0]
    n = len(widths) * len(STEPS)
    out = pl.pallas_call(
        functools.partial(share_kernel, widths=widths, offsets=offsets, half_cols=half_cols),
        in_specs=[SMEM, ANY],
        out_specs=[ANY] * n,
        out_shape=[jax.ShapeDtypeStruct((k, w), weight.dtype) for w in widths for _ in STEPS],
        scratch_shapes=[pltpu.SemaphoreType.DMA((n,))],
        name="weight_shares",
    )(pos, weight)
    return [out[g * len(STEPS):(g + 1) * len(STEPS)] for g in range(len(widths))]


def tile_kernel(pos_ref, w_ref, *refs, row_sizes, cols, offsets, half_cols, block):
    nr, nc = len(row_sizes), len(cols)
    a_refs, b_refs = refs[:4 * nr], refs[4 * nr:4 * nr + nc]
    outs = refs[4 * nr + nc:4 * nr + nc + NZ]
    a_v, b_v, sem_a, sem_b, sem_w = refs[4 * nr + nc + NZ:]
    width = w_ref.shape[0]
    total = sum(row_sizes)
    a_copies = []
    start = 0
    for i, tc in enumerate(row_sizes):
        for d in range(4):
            dst = a_v.at[:, :, pl.ds(start, tc), pl.ds(d * width, width)]
            a_copies.append(pltpu.make_async_copy(a_refs[4 * i + d], dst, sem_a.at[4 * i + d]))
        start += tc
    for c in a_copies:
        c.start()
    waits = []
    base = 0
    n = 0
    for g, (size, offset) in enumerate(zip(cols, offsets)):
        piece = size // (NX * NCORE)
        for start in range(0, size, block):
            here = []
            col = pl.multiple_of(lax.rem(pos_ref[0], 2) * half_cols + offset + start, LANES)
            nb = (base + start) // block
            here.append(pltpu.make_async_copy(
                w_ref.at[:, pl.ds(col, block)], b_v.at[pl.ds(0, width), pl.ds(base + start, block)], sem_w.at[nb]))
            for s in range(start // piece, (start + block) // piece):
                here.append(pltpu.make_async_copy(
                    b_refs[g].at[s], b_v.at[pl.ds(width, 3 * width), pl.ds(base + s * piece, piece)], sem_b.at[n]))
                n += 1
            for c in here:
                c.start()
            waits.append(here)
        base += size
    for c in a_copies:
        c.wait()
    a = a_v[...].reshape(NZ * 2 * total, 4 * width)
    for nb, here in enumerate(waits):
        for c in here:
            c.wait()
        at = pl.ds(nb * block, block)
        part = jnp.dot(a, b_v[:, at], preferred_element_type=jnp.float32).astype(jnp.bfloat16)
        part = part.reshape(NZ, 2, total, block)
        for zr in range(NZ):
            outs[zr][:, :, at] = part[zr]


def tile(pos, weight, a_parts, b_parts, cols, offsets, half_cols):
    width = weight.shape[0]
    row_sizes = tuple(a[0].shape[2] for a in a_parts)
    total, n = sum(row_sizes), sum(cols)
    block = 512
    flat = [piece for a in a_parts for piece in a]
    return pl.pallas_call(
        functools.partial(tile_kernel, row_sizes=row_sizes, cols=cols, offsets=offsets, half_cols=half_cols, block=block),
        in_specs=[SMEM, ANY] + [ANY] * (len(flat) + len(b_parts)),
        out_specs=[VMEM] * NZ,
        out_shape=[jax.ShapeDtypeStruct((2, total, n), jnp.bfloat16)] * NZ,
        scratch_shapes=[
            pltpu.VMEM((NZ, 2, total, 4 * width), jnp.bfloat16),
            pltpu.VMEM((4 * width, n), jnp.bfloat16),
            pltpu.SemaphoreType.DMA((len(flat),)),
            pltpu.SemaphoreType.DMA((NX * NCORE * len(cols),)),
            pltpu.SemaphoreType.DMA((n // block,)),
        ],
        compiler_params=LIMIT,
        cost_estimate=pl.CostEstimate(
            flops=2 * NZ * 2 * total * 4 * width * n, bytes_accessed=4 * width * n * 2 + NZ * 2 * total * n * 4, transcendentals=0),
        name="tile",
    )(pos, weight, *flat, *b_parts)


def place_kernel(pos_ref, *refs, places, half_cols):
    n = len(places)
    ins, out, sems = refs[:n], refs[n], refs[n + 1]
    copies = []
    for i, (other, row, rows, col, cols) in enumerate(places):
        half = lax.rem(pos_ref[0] + other, 2)
        at = pl.multiple_of(half * half_cols + col, LANES)
        copies.append(pltpu.make_async_copy(ins[i], out.at[pl.ds(row, rows), pl.ds(at, cols)], sems.at[i]))
    for c in copies:
        c.start()
    for c in copies:
        c.wait()


def local(query_proj, key_proj, value_proj, pole_rate, pole_residue, skip_gain, out_weight):
    rows, width = key_proj.shape
    owners = NY * NZ
    per = rows // owners
    total_cols = out_weight.shape[1]
    half_cols = total_cols // 2
    seq, chan = lax.axis_index("seq"), lax.axis_index("chan")
    my_y, my_z, core = chan // NZ, chan % NZ, seq % NCORE
    pos = jnp.stack([my_y, my_z, seq]).astype(jnp.int32)
    unit = per // sum(ROW_PARTS)
    tcs = [unit * n for n in ROW_PARTS]
    unit = half_cols // sum(COL_PARTS)
    cols = [unit * n for n in COL_PARTS]
    offsets = [sum(cols[:g]) for g in range(len(cols))]

    shares = weight_shares(pos, out_weight, [c // (NX * NCORE) for c in cols], offsets, half_cols)
    weights = []
    for group in shares:
        got = jnp.concatenate([over_y(piece, step) for piece, step in zip(group, STEPS)], axis=0)
        weights.append(lax.all_gather(got, "seq", axis=0))

    q3, k3, v3 = [x.reshape(owners, per, width) for x in (query_proj, key_proj, value_proj)]
    excl, span = states(k3, v3, pole_rate)
    across = jnp.exp(-pole_rate * rows)
    across2 = jnp.exp(-pole_rate * (2.0 * rows))
    across4 = jnp.exp(-pole_rate * (4.0 * rows))
    theirs = other_core(span)
    chip = jnp.where(core == 0, across * span + theirs, across * theirs + span)
    behind = from_chip_behind(chip, 1) + across2 * from_chip_behind(chip, 2) + across4 * from_chip_behind(chip, 3)
    incoming = jnp.where(core == 0, behind, across * behind + theirs)

    mixed = []
    state, start = excl, 0
    for i, tc in enumerate(tcs):
        sent, state = conv_chunk(
            pos, q3, k3, v3, pole_rate, pole_residue, skip_gain, state, incoming if i == 0 else None,
            start // tc, tc, i == len(tcs) - 1)
        mixed.append([sent[0]] + [over_y(piece, step) for piece, step in zip(sent[1:], STEPS)])
        start += tc

    pieces, places = [], []
    parity = my_y % 2
    for row_set, col_set in TILES:
        part = tile(
            pos, out_weight, [mixed[i] for i in row_set], [weights[g] for g in col_set],
            tuple(cols[g] for g in col_set), tuple(offsets[g] for g in col_set), half_cols)
        arrived = [part[0]] + [over_z(part[step % NZ], step) for step in STEPS]
        summed = sum(p.astype(jnp.float32) for p in arrived).astype(jnp.bfloat16)
        keep = lax.dynamic_index_in_dim(summed, parity, 0, keepdims=False)
        send = lax.dynamic_index_in_dim(summed, 1 - parity, 0, keepdims=False)
        row = sum(tcs[:row_set[0]])
        size = sum(tcs[i] for i in row_set)
        col = offsets[col_set[0]]
        n = sum(cols[g] for g in col_set)
        pieces += [keep, with_partner(send)]
        places += [(0, row, size, col, n), (1, row, size, col, n)]
    return pl.pallas_call(
        functools.partial(place_kernel, places=tuple(places), half_cols=half_cols),
        in_specs=[SMEM] + [ANY] * len(pieces),
        out_specs=ANY,
        out_shape=jax.ShapeDtypeStruct((per, total_cols), jnp.bfloat16),
        scratch_shapes=[pltpu.SemaphoreType.DMA((len(pieces),))],
        name="place",
    )(pos, *pieces)


def solution(mesh):
    in_specs = (
        P("seq", "chan"),
        P("seq", "chan"),
        P("seq", "chan"),
        P(None, "chan"),
        P(None, "chan"),
        P("chan"),
        P("chan", None),
    )
    out_specs = P(("seq", "chan"), None)
    return jax.shard_map(local, mesh=mesh, in_specs=in_specs, out_specs=out_specs, check_vma=False)
```

```python
import functools

import jax
import jax.numpy as jnp
from jax import lax
from jax.experimental import pallas as pl
from jax.experimental.pallas import tpu as pltpu
from jax.sharding import PartitionSpec as P

POLES = 16
LANES = 128
NX, NCORE, NY, NZ = 4, 2, 4, 4
STEPS = (1, -1, 2)
ROW_PARTS = (1, 1)
COL_PARTS = (1, 1)
TILES = (((0,), (0,)), ((1,), (0,)), ((0,), (1,)), ((1,), (1,)))
HBM = pl.BlockSpec(memory_space=pltpu.HBM)
SMEM = pl.BlockSpec(memory_space=pltpu.SMEM)
VMEM = pl.BlockSpec(memory_space=pltpu.VMEM)
LIMIT = pltpu.CompilerParams(vmem_limit_bytes=48 * 1024 * 1024)


def over_y(value, step):
    return lax.ppermute(value, "chan", [(y * NZ + z, (y + step) % NY * NZ + z) for y in range(NY) for z in range(NZ)])


def over_z(value, step):
    return lax.ppermute(value, "chan", [(y * NZ + z, y * NZ + (z + step) % NZ) for y in range(NY) for z in range(NZ)])


def with_partner(value):
    return lax.ppermute(value, "chan", [(y * NZ + z, (y ^ 1) * NZ + z) for y in range(NY) for z in range(NZ)])


def other_core(value):
    return lax.ppermute(value, "seq", [(s, s ^ 1) for s in range(NX * NCORE)])


def from_chip_behind(value, step):
    pairs = [(x * NCORE + c, (x + step) * NCORE + c) for x in range(NX - step) for c in range(NCORE)]
    return lax.ppermute(value, "seq", pairs)


def state_kernel(k_ref, v_ref, rate_ref, excl_ref, span_ref, drive, fb, *, T, unroll):
    W = k_ref.shape[-1]
    nO = k_ref.shape[0]
    drive[...] = (k_ref[...].astype(jnp.float32) * v_ref[...].astype(jnp.float32)).reshape(nO*T, W)
    rate = rate_ref[...]
    f = jnp.exp(-rate)
    for r in range(POLES):
        fb[r] = jnp.broadcast_to(f[r:r+1], (8, W))
    oid = lax.broadcasted_iota(jnp.int32, (8, W), 0)
    prev = None
    fT = jnp.exp(-rate * T)
    finals = []
    G = nO//8
    fr = [fb[r] for r in range(POLES)]
    def body(i, s):
        s = [list(x) for x in s]
        for j in range(unroll):
            for p in range(G):
                u = drive[pl.ds(p*8*T + i*unroll + j, 8, stride=T), :]
                for r in range(POLES):
                    s[p][r] = fr[r]*s[p][r] + u
        return tuple(tuple(x) for x in s)
    finals = lax.fori_loop(0, T//unroll, body, tuple(tuple(jnp.zeros((8,W),jnp.float32) for _ in range(POLES)) for p in range(G)))
    spans=[]
    for r in range(POLES):
        carry = jnp.zeros((1,W),jnp.float32)
        g = fT[r:r+1]
        g2 = g*g; g4 = g2*g2; g8 = g4*g4
        pw = jnp.ones((8,W),jnp.float32)
        pw = jnp.where((oid & 1)!=0, pw*g, pw)
        pw = jnp.where((oid & 2)!=0, pw*g2, pw)
        pw = jnp.where((oid & 4)!=0, pw*g4, pw)
        for p in range(nO//8):
            s = finals[p][r]
            for d, gd in ((1,g),(2,g2),(4,g4)):
                s = s + jnp.where(oid>=d, pltpu.roll(s, d, 0), 0.0)*gd
            ex = jnp.where(oid>=1, pltpu.roll(s,1,0), 0.0) + pw*carry
            excl_ref[r, pl.ds(p*8,8), :] = ex
            carry = s[7:8] + g8*carry
        spans.append(carry)
    span_ref[...] = jnp.concatenate(spans, axis=0)

def states(k3, v3, rate, unroll=4):
    nO,T,C = k3.shape
    W=128
    return pl.pallas_call(
        functools.partial(state_kernel, T=T, unroll=unroll),
        grid=(C//W,),
        in_specs=[pl.BlockSpec((nO,T,W), lambda c:(0,0,c)), pl.BlockSpec((nO,T,W), lambda c:(0,0,c)),
                  pl.BlockSpec((POLES,W), lambda c:(0,c))],
        out_specs=[pl.BlockSpec((POLES,nO,W), lambda c:(0,0,c)), pl.BlockSpec((POLES,W), lambda c:(0,c))],
        out_shape=[jax.ShapeDtypeStruct((POLES,nO,C), jnp.float32), jax.ShapeDtypeStruct((POLES,C), jnp.float32)],
        scratch_shapes=[pltpu.VMEM((nO*T,W), jnp.float32), pltpu.VMEM((POLES,8,W), jnp.float32)],
        name="states",
    )(k3, v3, rate)


def conv_kernel(pos_ref, q_ref, k_ref, v_ref, rate_ref, res_ref, skip_ref, init_ref, *rest, unroll, per, first, last):
    rest = list(rest)
    inc_ref = rest.pop(0) if first else None
    outs = rest[:4]
    state_ref = None if last else rest[4]
    drive, y, fb, rb, mixed = rest[4 if last else 5:]
    nO, T, W = k_ref.shape
    drive[...] = (k_ref[...].astype(jnp.float32) * v_ref[...].astype(jnp.float32)).reshape(nO * T, W)
    rate = rate_ref[...]
    f = jnp.exp(-rate)
    for r in range(POLES):
        fb[r] = jnp.broadcast_to(f[r:r + 1], (8, W))
        rb[r] = jnp.broadcast_to(res_ref[r:r + 1], (8, W))
    rb[POLES] = jnp.broadcast_to(skip_ref[...], (8, W))
    fr = [fb[r] for r in range(POLES)]
    G = nO // 8

    def begin(p, r):
        s = init_ref[r, pl.ds(p * 8, 8), :]
        if first:
            owner = (lax.broadcasted_iota(jnp.int32, (8, W), 0) + p * 8).astype(jnp.float32)
            s = s + jnp.exp(-(rate[r:r + 1] * float(per)) * owner) * inc_ref[r:r + 1]
        return s

    def body(i, s):
        s = [list(x) for x in s]
        for j in range(unroll):
            t = i * unroll + j
            us = [drive[pl.ds(p * 8 * T + t, 8, stride=T), :] for p in range(G)]
            acc = [[rb[POLES] * us[p], None] for p in range(G)]
            for r in range(POLES):
                rr = rb[r]
                for p in range(G):
                    s[p][r] = fr[r] * s[p][r] + us[p]
                    m = rr * s[p][r]
                    acc[p][r % 2] = m if acc[p][r % 2] is None else acc[p][r % 2] + m
            for p in range(G):
                y[pl.ds(p * 8 * T + t, 8, stride=T), :] = acc[p][0] + acc[p][1]
        return tuple(tuple(x) for x in s)

    s = lax.fori_loop(0, T // unroll, body, tuple(tuple(begin(p, r) for r in range(POLES)) for p in range(G)))
    if not last:
        for p in range(G):
            for r in range(POLES):
                state_ref[r, pl.ds(p * 8, 8), :] = s[p][r]
    mixed[...] = (q_ref[...].astype(jnp.float32) * y[...].reshape(nO, T, W)).astype(jnp.bfloat16)
    my_y, my_z = pos_ref[0], pos_ref[1]
    for out_ref, step in zip(outs, (0,) + STEPS):
        half = lax.rem(my_y + step + NY, NY) // 2
        for zr in range(NZ):
            z = lax.rem(my_z + zr, NZ)
            for yl in range(2):
                out_ref[zr, yl] = mixed[half * 8 + yl * NZ + z]


def conv_chunk(pos, q3, k3, v3, rate, res, skip, init, inc, index, tc, last):
    nO, T, C = k3.shape
    W = LANES
    first = inc is not None
    row = pl.BlockSpec((nO, tc, W), lambda c: (0, index, c))
    par = pl.BlockSpec((POLES, W), lambda c: (0, c))
    st = pl.BlockSpec((POLES, nO, W), lambda c: (0, 0, c))
    ops = [pos, q3, k3, v3, rate, res, skip.reshape(1, -1), init]
    specs = [SMEM, row, row, row, par, par, pl.BlockSpec((1, W), lambda c: (0, c)), st]
    if first:
        ops.append(inc)
        specs.append(par)
    out = pltpu.HBM((NZ, 2, tc, C), jnp.bfloat16)
    out_shape = [out] * 4
    out_specs = [pl.BlockSpec((NZ, 2, tc, W), lambda c: (0, 0, 0, c))] * 4
    if not last:
        out_shape = out_shape + [jax.ShapeDtypeStruct((POLES, nO, C), jnp.float32)]
        out_specs = out_specs + [st]
    res = pl.pallas_call(
        functools.partial(conv_kernel, unroll=4, per=T, first=first, last=last),
        grid=(C // W,),
        in_specs=specs,
        out_specs=out_specs,
        out_shape=out_shape,
        scratch_shapes=[
            pltpu.VMEM((nO * tc, W), jnp.float32),
            pltpu.VMEM((nO * tc, W), jnp.float32),
            pltpu.VMEM((POLES, 8, W), jnp.float32),
            pltpu.VMEM((POLES + 1, 8, W), jnp.float32),
            pltpu.VMEM((nO, tc, W), jnp.bfloat16),
        ],
        compiler_params=LIMIT,
        cost_estimate=pl.CostEstimate(flops=nO * tc * C * POLES * 4, bytes_accessed=nO * tc * C * 10, transcendentals=0),
        name="conv",
    )(*ops)
    return res[:4], (None if last else res[4])


def share_kernel(pos_ref, w_ref, *refs, widths, offsets, half_cols):
    n = len(widths) * len(STEPS)
    outs, sems = refs[:n], refs[n]
    copies = []
    for g, (width, offset) in enumerate(zip(widths, offsets)):
        for i, step in enumerate(STEPS):
            half = lax.rem(lax.rem(pos_ref[0] + step + NY, NY), 2)
            col = pl.multiple_of(half * half_cols + offset + pos_ref[2] * width, LANES)
            k = g * len(STEPS) + i
            copies.append(pltpu.make_async_copy(w_ref.at[:, pl.ds(col, width)], outs[k], sems.at[k]))
    for c in copies:
        c.start()
    for c in copies:
        c.wait()


def weight_shares(pos, weight, widths, offsets, half_cols):
    k = weight.shape[0]
    n = len(widths) * len(STEPS)
    out = pl.pallas_call(
        functools.partial(share_kernel, widths=widths, offsets=offsets, half_cols=half_cols),
        in_specs=[SMEM, HBM],
        out_specs=[VMEM] * n,
        out_shape=[pltpu.HBM((k, w), weight.dtype) for w in widths for _ in STEPS],
        scratch_shapes=[pltpu.SemaphoreType.DMA((n,))],
        compiler_params=LIMIT,
        name="weight_shares",
    )(pos, weight)
    return [out[g * len(STEPS):(g + 1) * len(STEPS)] for g in range(len(widths))]


def tile_kernel(pos_ref, w_ref, *refs, row_sizes, cols, offsets, half_cols, block):
    nr, nc = len(row_sizes), len(cols)
    a_refs, b_refs = refs[:4 * nr], refs[4 * nr:4 * nr + nc]
    outs = refs[4 * nr + nc:4 * nr + nc + NZ]
    a_v, b_v, sem_a, sem_b, sem_w = refs[4 * nr + nc + NZ:]
    width = w_ref.shape[0]
    total = sum(row_sizes)
    a_copies = []
    start = 0
    for i, tc in enumerate(row_sizes):
        for d in range(4):
            dst = a_v.at[:, :, pl.ds(start, tc), pl.ds(d * width, width)]
            a_copies.append(pltpu.make_async_copy(a_refs[4 * i + d], dst, sem_a.at[4 * i + d]))
        start += tc
    for c in a_copies:
        c.start()
    waits = []
    base = 0
    n = 0
    for g, (size, offset) in enumerate(zip(cols, offsets)):
        piece = size // (NX * NCORE)
        for start in range(0, size, block):
            here = []
            col = pl.multiple_of(lax.rem(pos_ref[0], 2) * half_cols + offset + start, LANES)
            nb = (base + start) // block
            here.append(pltpu.make_async_copy(
                w_ref.at[:, pl.ds(col, block)], b_v.at[pl.ds(0, width), pl.ds(base + start, block)], sem_w.at[nb]))
            for s in range(start // piece, (start + block) // piece):
                here.append(pltpu.make_async_copy(
                    b_refs[g].at[s], b_v.at[pl.ds(width, 3 * width), pl.ds(base + s * piece, piece)], sem_b.at[n]))
                n += 1
            for c in here:
                c.start()
            waits.append(here)
        base += size
    for c in a_copies:
        c.wait()
    a = a_v[...].reshape(NZ * 2 * total, 4 * width)
    for nb, here in enumerate(waits):
        for c in here:
            c.wait()
        at = pl.ds(nb * block, block)
        part = jnp.dot(a, b_v[:, at], preferred_element_type=jnp.float32).astype(jnp.bfloat16)
        part = part.reshape(NZ, 2, total, block)
        for zr in range(NZ):
            outs[zr][:, :, at] = part[zr]


def tile(pos, weight, a_parts, b_parts, cols, offsets, half_cols):
    width = weight.shape[0]
    row_sizes = tuple(a[0].shape[2] for a in a_parts)
    total, n = sum(row_sizes), sum(cols)
    block = 512
    flat = [piece for a in a_parts for piece in a]
    return pl.pallas_call(
        functools.partial(tile_kernel, row_sizes=row_sizes, cols=cols, offsets=offsets, half_cols=half_cols, block=block),
        in_specs=[SMEM, HBM] + [HBM] * (len(flat) + len(b_parts)),
        out_specs=[VMEM] * NZ,
        out_shape=[pltpu.HBM((2, total, n), jnp.bfloat16)] * NZ,
        scratch_shapes=[
            pltpu.VMEM((NZ, 2, total, 4 * width), jnp.bfloat16),
            pltpu.VMEM((4 * width, n), jnp.bfloat16),
            pltpu.SemaphoreType.DMA((len(flat),)),
            pltpu.SemaphoreType.DMA((NX * NCORE * len(cols),)),
            pltpu.SemaphoreType.DMA((n // block,)),
        ],
        compiler_params=LIMIT,
        cost_estimate=pl.CostEstimate(
            flops=2 * NZ * 2 * total * 4 * width * n, bytes_accessed=4 * width * n * 2 + NZ * 2 * total * n * 4, transcendentals=0),
        name="tile",
    )(pos, weight, *flat, *b_parts)


def place_kernel(pos_ref, *refs, places, half_cols):
    n = len(places)
    ins, out, sems = refs[:n], refs[n], refs[n + 1]
    copies = []
    for i, (other, row, rows, col, cols) in enumerate(places):
        half = lax.rem(pos_ref[0] + other, 2)
        at = pl.multiple_of(half * half_cols + col, LANES)
        copies.append(pltpu.make_async_copy(ins[i], out.at[pl.ds(row, rows), pl.ds(at, cols)], sems.at[i]))
    for c in copies:
        c.start()
    for c in copies:
        c.wait()


def local(query_proj, key_proj, value_proj, pole_rate, pole_residue, skip_gain, out_weight):
    rows, width = key_proj.shape
    owners = NY * NZ
    per = rows // owners
    total_cols = out_weight.shape[1]
    half_cols = total_cols // 2
    seq, chan = lax.axis_index("seq"), lax.axis_index("chan")
    my_y, my_z, core = chan // NZ, chan % NZ, seq % NCORE
    pos = jnp.stack([my_y, my_z, seq]).astype(jnp.int32)
    unit = per // sum(ROW_PARTS)
    tcs = [unit * n for n in ROW_PARTS]
    unit = half_cols // sum(COL_PARTS)
    cols = [unit * n for n in COL_PARTS]
    offsets = [sum(cols[:g]) for g in range(len(cols))]

    shares = weight_shares(pos, out_weight, [c // (NX * NCORE) for c in cols], offsets, half_cols)
    fetched = [[over_y(piece, step) for piece, step in zip(group, STEPS)] for group in shares]

    q3, k3, v3 = [x.reshape(owners, per, width) for x in (query_proj, key_proj, value_proj)]
    excl, span = states(k3, v3, pole_rate)

    def gathered(group, after):
        _, *pieces = lax.optimization_barrier((after, *group))
        return lax.all_gather(jnp.concatenate(pieces, axis=0), "seq", axis=0)

    weights = [gathered(fetched[0], span)]
    across = jnp.exp(-pole_rate * rows)
    across2 = jnp.exp(-pole_rate * (2.0 * rows))
    across4 = jnp.exp(-pole_rate * (4.0 * rows))
    theirs = other_core(span)
    chip = jnp.where(core == 0, across * span + theirs, across * theirs + span)
    behind = from_chip_behind(chip, 1) + across2 * from_chip_behind(chip, 2) + across4 * from_chip_behind(chip, 3)
    incoming = jnp.where(core == 0, behind, across * behind + theirs)

    mixed = []
    state, start = excl, 0
    for i, tc in enumerate(tcs):
        sent, state = conv_chunk(
            pos, q3, k3, v3, pole_rate, pole_residue, skip_gain, state, incoming if i == 0 else None,
            start // tc, tc, i == len(tcs) - 1)
        if i + 1 < len(fetched):
            weights.append(gathered(fetched[i + 1], sent[0]))
        mixed.append([sent[0]] + [over_y(piece, step) for piece, step in zip(sent[1:], STEPS)])
        start += tc

    pieces, places = [], []
    parity = my_y % 2
    for row_set, col_set in TILES:
        part = tile(
            pos, out_weight, [mixed[i] for i in row_set], [weights[g] for g in col_set],
            tuple(cols[g] for g in col_set), tuple(offsets[g] for g in col_set), half_cols)
        arrived = [part[0]] + [over_z(part[step % NZ], step) for step in STEPS]
        summed = sum(p.astype(jnp.float32) for p in arrived).astype(jnp.bfloat16)
        keep = lax.dynamic_index_in_dim(summed, parity, 0, keepdims=False)
        send = lax.dynamic_index_in_dim(summed, 1 - parity, 0, keepdims=False)
        row = sum(tcs[:row_set[0]])
        size = sum(tcs[i] for i in row_set)
        col = offsets[col_set[0]]
        n = sum(cols[g] for g in col_set)
        pieces += [keep, with_partner(send)]
        places += [(0, row, size, col, n), (1, row, size, col, n)]
    return pl.pallas_call(
        functools.partial(place_kernel, places=tuple(places), half_cols=half_cols),
        in_specs=[SMEM] + [HBM] * len(pieces),
        out_specs=VMEM,
        out_shape=jax.ShapeDtypeStruct((per, total_cols), jnp.bfloat16),
        scratch_shapes=[pltpu.SemaphoreType.DMA((len(pieces),))],
        compiler_params=LIMIT,
        name="place",
    )(pos, *pieces)


def solution(mesh):
    in_specs = (
        P("seq", "chan"),
        P("seq", "chan"),
        P("seq", "chan"),
        P(None, "chan"),
        P(None, "chan"),
        P("chan"),
        P("chan", None),
    )
    out_specs = P(("seq", "chan"), None)
    return jax.shard_map(local, mesh=mesh, in_specs=in_specs, out_specs=out_specs, check_vma=False)
```

```python
import functools

import jax
import jax.numpy as jnp
from jax import lax
from jax.experimental import pallas as pl
from jax.experimental.pallas import tpu as pltpu
from jax.sharding import PartitionSpec as P

POLES = 16
PAD = 8
LANES = 128
NX, NCORE, NY, NZ = 4, 2, 4, 4
STEPS = (1, -1, 2)
ROW_PARTS = (1, 1)
COL_PARTS = (1, 1)
TILES = (((0,), (0,)), ((1,), (0,)), ((0,), (1,)), ((1,), (1,)))
OFFLOADED = ()
HBM = pl.BlockSpec(memory_space=pltpu.HBM)
SMEM = pl.BlockSpec(memory_space=pltpu.SMEM)
VMEM = pl.BlockSpec(memory_space=pltpu.VMEM)
LIMIT = pltpu.CompilerParams(vmem_limit_bytes=60 * 1024 * 1024)


def work(us):
    return pl.CostEstimate(flops=us * 1_150_000_000, bytes_accessed=0, transcendentals=0)


def over_y(value, step):
    return lax.ppermute(value, "chan", [(y * NZ + z, (y + step) % NY * NZ + z) for y in range(NY) for z in range(NZ)])


def over_z(value, step):
    return lax.ppermute(value, "chan", [(y * NZ + z, y * NZ + (z + step) % NZ) for y in range(NY) for z in range(NZ)])


def with_partner(value):
    return lax.ppermute(value, "chan", [(y * NZ + z, (y ^ 1) * NZ + z) for y in range(NY) for z in range(NZ)])


def other_core(value):
    return lax.ppermute(value, "seq", [(s, s ^ 1) for s in range(NX * NCORE)])


def from_chip_behind(value, step):
    pairs = [(x * NCORE + c, (x + step) * NCORE + c) for x in range(NX - step) for c in range(NCORE)]
    return lax.ppermute(value, "seq", pairs)


def state_kernel(k_ref, v_ref, rate_ref, excl_ref, span_ref, drive, fb, *, T, unroll):
    W = k_ref.shape[-1]
    nO = k_ref.shape[0]
    PT = T + PAD
    for o in range(nO):
        drive[pl.ds(o*PT, T), :] = k_ref[o].astype(jnp.float32) * v_ref[o].astype(jnp.float32)
    rate = rate_ref[...]
    f = jnp.exp(-rate)
    for r in range(POLES):
        fb[r] = jnp.broadcast_to(f[r:r+1], (8, W))
    oid = lax.broadcasted_iota(jnp.int32, (8, W), 0)
    prev = None
    fT = jnp.exp(-rate * T)
    finals = []
    G = nO//8
    fr = [fb[r] for r in range(POLES)]
    def body(i, s):
        s = [list(x) for x in s]
        for j in range(unroll):
            for p in range(G):
                u = drive[pl.ds(p*8*PT + i*unroll + j, 8, stride=PT), :]
                for r in range(POLES):
                    s[p][r] = fr[r]*s[p][r] + u
        return tuple(tuple(x) for x in s)
    finals = lax.fori_loop(0, T//unroll, body, tuple(tuple(jnp.zeros((8,W),jnp.float32) for _ in range(POLES)) for p in range(G)))
    spans=[]
    for r in range(POLES):
        carry = jnp.zeros((1,W),jnp.float32)
        g = fT[r:r+1]
        g2 = g*g; g4 = g2*g2; g8 = g4*g4
        pw = jnp.ones((8,W),jnp.float32)
        pw = jnp.where((oid & 1)!=0, pw*g, pw)
        pw = jnp.where((oid & 2)!=0, pw*g2, pw)
        pw = jnp.where((oid & 4)!=0, pw*g4, pw)
        for p in range(nO//8):
            s = finals[p][r]
            for d, gd in ((1,g),(2,g2),(4,g4)):
                s = s + jnp.where(oid>=d, pltpu.roll(s, d, 0), 0.0)*gd
            ex = jnp.where(oid>=1, pltpu.roll(s,1,0), 0.0) + pw*carry
            excl_ref[r, pl.ds(p*8,8), :] = ex
            carry = s[7:8] + g8*carry
        spans.append(carry)
    span_ref[...] = jnp.concatenate(spans, axis=0)

def states(k3, v3, rate, unroll=16):
    nO,T,C = k3.shape
    W=128
    return pl.pallas_call(
        functools.partial(state_kernel, T=T, unroll=unroll),
        grid=(C//W,),
        in_specs=[pl.BlockSpec((nO,T,W), lambda c:(0,0,c)), pl.BlockSpec((nO,T,W), lambda c:(0,0,c)),
                  pl.BlockSpec((POLES,W), lambda c:(0,c))],
        out_specs=[pl.BlockSpec((POLES,nO,W), lambda c:(0,0,c)), pl.BlockSpec((POLES,W), lambda c:(0,c))],
        out_shape=[jax.ShapeDtypeStruct((POLES,nO,C), jnp.float32), jax.ShapeDtypeStruct((POLES,C), jnp.float32)],
        scratch_shapes=[pltpu.VMEM((nO*(T+PAD),W), jnp.float32), pltpu.VMEM((POLES,8,W), jnp.float32)],
        compiler_params=LIMIT,
        cost_estimate=work(8),
        name="states",
    )(k3, v3, rate)


def conv_kernel(pos_ref, q_ref, k_ref, v_ref, rate_ref, res_ref, skip_ref, init_ref, *rest, unroll, per, first, last):
    rest = list(rest)
    inc_ref = rest.pop(0) if first else None
    outs = rest[:4]
    state_ref = None if last else rest[4]
    drive, y, fb, rb, mixed = rest[4 if last else 5:]
    nO, T, W = k_ref.shape
    PT = T + PAD
    for o in range(nO):
        drive[pl.ds(o * PT, T), :] = k_ref[o].astype(jnp.float32) * v_ref[o].astype(jnp.float32)
    rate = rate_ref[...]
    f = jnp.exp(-rate)
    for r in range(POLES):
        fb[r] = jnp.broadcast_to(f[r:r + 1], (8, W))
        rb[r] = jnp.broadcast_to(res_ref[r:r + 1], (8, W))
    rb[POLES] = jnp.broadcast_to(skip_ref[...], (8, W))
    fr = [fb[r] for r in range(POLES)]
    G = nO // 8

    def begin(p, r):
        s = init_ref[r, pl.ds(p * 8, 8), :]
        if first:
            owner = (lax.broadcasted_iota(jnp.int32, (8, W), 0) + p * 8).astype(jnp.float32)
            s = s + jnp.exp(-(rate[r:r + 1] * float(per)) * owner) * inc_ref[r:r + 1]
        return s

    def body(i, s):
        s = [list(x) for x in s]
        for j in range(unroll):
            t = i * unroll + j
            us = [drive[pl.ds(p * 8 * PT + t, 8, stride=PT), :] for p in range(G)]
            acc = [[rb[POLES] * us[p], None] for p in range(G)]
            for r in range(POLES):
                rr = rb[r]
                for p in range(G):
                    s[p][r] = fr[r] * s[p][r] + us[p]
                    m = rr * s[p][r]
                    acc[p][r % 2] = m if acc[p][r % 2] is None else acc[p][r % 2] + m
            for p in range(G):
                y[pl.ds(p * 8 * PT + t, 8, stride=PT), :] = acc[p][0] + acc[p][1]
        return tuple(tuple(x) for x in s)

    s = lax.fori_loop(0, T // unroll, body, tuple(tuple(begin(p, r) for r in range(POLES)) for p in range(G)))
    if not last:
        for p in range(G):
            for r in range(POLES):
                state_ref[r, pl.ds(p * 8, 8), :] = s[p][r]
    for o in range(nO):
        mixed[o] = (q_ref[o].astype(jnp.float32) * y[pl.ds(o * PT, T), :]).astype(jnp.bfloat16)
    my_y, my_z = pos_ref[0], pos_ref[1]
    for out_ref, step in zip(outs, (0,) + STEPS):
        half = lax.rem(my_y + step + NY, NY) // 2
        for zr in range(NZ):
            z = lax.rem(my_z + zr, NZ)
            for yl in range(2):
                out_ref[zr, yl] = mixed[half * 8 + yl * NZ + z]


def conv_chunk(pos, q3, k3, v3, rate, res, skip, init, inc, index, tc, last):
    nO, T, C = k3.shape
    W = LANES
    first = inc is not None
    row = pl.BlockSpec((nO, tc, W), lambda c: (0, index, c))
    par = pl.BlockSpec((POLES, W), lambda c: (0, c))
    st = pl.BlockSpec((POLES, nO, W), lambda c: (0, 0, c))
    ops = [pos, q3, k3, v3, rate, res, skip.reshape(1, -1), init]
    specs = [SMEM, row, row, row, par, par, pl.BlockSpec((1, W), lambda c: (0, c)), st]
    if first:
        ops.append(inc)
        specs.append(par)
    out = pltpu.HBM((NZ, 2, tc, C), jnp.bfloat16)
    out_shape = [out] * 4
    out_specs = [pl.BlockSpec((NZ, 2, tc, W), lambda c: (0, 0, 0, c))] * 4
    if not last:
        out_shape = out_shape + [jax.ShapeDtypeStruct((POLES, nO, C), jnp.float32)]
        out_specs = out_specs + [st]
    res = pl.pallas_call(
        functools.partial(conv_kernel, unroll=16, per=T, first=first, last=last),
        grid=(C // W,),
        in_specs=specs,
        out_specs=out_specs,
        out_shape=out_shape,
        scratch_shapes=[
            pltpu.VMEM((nO * (tc + PAD), W), jnp.float32),
            pltpu.VMEM((nO * (tc + PAD), W), jnp.float32),
            pltpu.VMEM((POLES, 8, W), jnp.float32),
            pltpu.VMEM((POLES + 1, 8, W), jnp.float32),
            pltpu.VMEM((nO, tc, W), jnp.bfloat16),
        ],
        compiler_params=LIMIT,
        cost_estimate=work(8),
        name="conv",
    )(*ops)
    return res[:4], (None if last else res[4])


def share_kernel(pos_ref, w_ref, *refs, widths, offsets, half_cols):
    n = len(widths) * len(STEPS)
    outs, sems = refs[:n], refs[n]
    copies = []
    for g, (width, offset) in enumerate(zip(widths, offsets)):
        for i, step in enumerate(STEPS):
            half = lax.rem(lax.rem(pos_ref[0] + step + NY, NY), 2)
            col = pl.multiple_of(half * half_cols + offset + pos_ref[2] * width, LANES)
            k = g * len(STEPS) + i
            copies.append(pltpu.make_async_copy(w_ref.at[:, pl.ds(col, width)], outs[k], sems.at[k]))
    for c in copies:
        c.start()
    for c in copies:
        c.wait()


def weight_shares(pos, weight, widths, offsets, half_cols):
    k = weight.shape[0]
    n = len(widths) * len(STEPS)
    out = pl.pallas_call(
        functools.partial(share_kernel, widths=widths, offsets=offsets, half_cols=half_cols),
        in_specs=[SMEM, HBM],
        out_specs=[VMEM] * n,
        out_shape=[jax.ShapeDtypeStruct((k, w), weight.dtype) for w in widths for _ in STEPS],
        scratch_shapes=[pltpu.SemaphoreType.DMA((n,))],
        compiler_params=LIMIT,
        name="weight_shares",
    )(pos, weight)
    return [out[g * len(STEPS):(g + 1) * len(STEPS)] for g in range(len(widths))]


def tile_kernel(pos_ref, w_ref, *refs, row_sizes, cols, offsets, half_cols, block, split):
    nr, nc = len(row_sizes), len(cols)
    a_refs, b_refs = refs[:4 * nr], refs[4 * nr:4 * nr + nc]
    n_out = 1 if split else NZ
    outs = refs[4 * nr + nc:4 * nr + nc + n_out]
    a_v, b_v, out_v, sem_a, sem_b, sem_w, sem_out = refs[4 * nr + nc + n_out:]
    width = w_ref.shape[0]
    total = sum(row_sizes)
    a_copies = []
    start = 0
    for i, tc in enumerate(row_sizes):
        for d in range(4):
            dst = a_v.at[:, :, pl.ds(start, tc), pl.ds(d * width, width)]
            a_copies.append(pltpu.make_async_copy(a_refs[4 * i + d], dst, sem_a.at[4 * i + d]))
        start += tc
    blocks = []
    base = 0
    n = 0
    for g, (size, offset) in enumerate(zip(cols, offsets)):
        piece = size // (NX * NCORE)
        for start in range(0, size, block):
            here = []
            col = pl.multiple_of(lax.rem(pos_ref[0], 2) * half_cols + offset + start, LANES)
            nb = (base + start) // block
            here.append(pltpu.make_async_copy(
                w_ref.at[:, pl.ds(col, block)], b_v.at[pl.ds(0, width), pl.ds(base + start, block)], sem_w.at[nb]))
            for s in range(start // piece, (start + block) // piece):
                here.append(pltpu.make_async_copy(
                    b_refs[g].at[s], b_v.at[pl.ds(width, 3 * width), pl.ds(base + s * piece, piece)], sem_b.at[n]))
                n += 1
            blocks.append(here)
        base += size

    def begin(nb):
        if nb < len(blocks):
            for c in blocks[nb]:
                c.start()

    for c in a_copies:
        c.start()
    begin(0)
    for c in a_copies:
        c.wait()
    begin(1)
    begin(2)
    out_copies = []
    a = a_v[...].reshape(NZ * 2 * total, 4 * width)
    for nb, here in enumerate(blocks):
        for c in here:
            c.wait()
        begin(nb + 3)
        at = pl.ds(nb * block, block)
        part = jnp.dot(a, b_v[:, at], preferred_element_type=jnp.float32).astype(jnp.bfloat16)
        out_v[:, :, :, at] = part.reshape(NZ, 2, total, block)
        for zr in range(NZ):
            pairs = []
            for i in range(2):
                src = out_v.at[zr, lax.rem(pos_ref[0] + 1 + i, 2), :, at]
                dst = outs[0].at[lax.rem(pos_ref[1] + zr, NZ), i, :, at] if split else outs[zr].at[i, :, at]
                pairs.append((src, dst))
            for src, dst in pairs:
                c = pltpu.make_async_copy(src, dst, sem_out.at[len(out_copies)])
                c.start()
                out_copies.append(c)
    for c in out_copies:
        c.wait()


def tile(pos, weight, a_parts, b_parts, cols, offsets, half_cols, split):
    width = weight.shape[0]
    row_sizes = tuple(a[0].shape[2] for a in a_parts)
    total, n = sum(row_sizes), sum(cols)
    block = 512
    flat = [piece for a in a_parts for piece in a]
    outs = [pltpu.HBM((NZ, 2, total, n), jnp.bfloat16)] if split else [pltpu.HBM((2, total, n), jnp.bfloat16)] * NZ
    return pl.pallas_call(
        functools.partial(tile_kernel, row_sizes=row_sizes, cols=cols, offsets=offsets, half_cols=half_cols, block=block, split=split),
        in_specs=[SMEM, HBM] + [HBM] * (len(flat) + len(b_parts)),
        out_specs=[HBM] * len(outs),
        out_shape=outs,
        scratch_shapes=[
            pltpu.VMEM((NZ, 2, total, 4 * width), jnp.bfloat16),
            pltpu.VMEM((4 * width, n), jnp.bfloat16),
            pltpu.VMEM((NZ, 2, total, n), jnp.bfloat16),
            pltpu.SemaphoreType.DMA((len(flat),)),
            pltpu.SemaphoreType.DMA((NX * NCORE * len(cols),)),
            pltpu.SemaphoreType.DMA((n // block,)),
            pltpu.SemaphoreType.DMA((n // block * 2 * NZ,)),
        ],
        compiler_params=LIMIT,
        cost_estimate=work(9),
        name="tile",
    )(pos, weight, *flat, *b_parts)


def place_kernel(pos_ref, *refs, places, half_cols):
    n = len(places)
    ins, out, sems = refs[:n], refs[n], refs[n + 1]
    copies = []
    for i, (other, row, rows, col, cols) in enumerate(places):
        at = pl.multiple_of(lax.rem(pos_ref[0] + other, 2) * half_cols + col, LANES)
        copies.append(pltpu.make_async_copy(ins[i], out.at[pl.ds(row, rows), pl.ds(at, cols)], sems.at[i]))
    for c in copies:
        c.start()
    for c in copies:
        c.wait()


def place(pos, pieces, places, shape, half_cols):
    return pl.pallas_call(
        functools.partial(place_kernel, places=tuple(places), half_cols=half_cols),
        in_specs=[SMEM] + [pl.BlockSpec(memory_space=pl.ANY)] * len(pieces),
        out_specs=VMEM,
        out_shape=jax.ShapeDtypeStruct(shape, jnp.bfloat16),
        scratch_shapes=[pltpu.SemaphoreType.DMA((len(pieces),))],
        compiler_params=pltpu.CompilerParams(vmem_limit_bytes=32 * 1024 * 1024),
        name="place",
    )(pos, *pieces)


def local(query_proj, key_proj, value_proj, pole_rate, pole_residue, skip_gain, out_weight):
    rows, width = key_proj.shape
    owners = NY * NZ
    per = rows // owners
    total_cols = out_weight.shape[1]
    half_cols = total_cols // 2
    seq, chan = lax.axis_index("seq"), lax.axis_index("chan")
    my_y, my_z, core = chan // NZ, chan % NZ, seq % NCORE
    pos = jnp.stack([my_y, my_z, seq]).astype(jnp.int32)
    unit = per // sum(ROW_PARTS)
    tcs = [unit * n for n in ROW_PARTS]
    unit = half_cols // sum(COL_PARTS)
    cols = [unit * n for n in COL_PARTS]
    offsets = [sum(cols[:g]) for g in range(len(cols))]

    shares = weight_shares(pos, out_weight, [c // (NX * NCORE) for c in cols], offsets, half_cols)
    fetched = [[over_y(piece, step) for piece, step in zip(group, STEPS)] for group in shares]

    q3, k3, v3 = [x.reshape(owners, per, width) for x in (query_proj, key_proj, value_proj)]
    k3 = lax.optimization_barrier((k3, shares[0][0]))[0]
    excl, span = states(k3, v3, pole_rate)

    def gathered(group, after):
        _, *pieces = lax.optimization_barrier((after, *group))
        return lax.all_gather(jnp.concatenate(pieces, axis=0), "seq", axis=0)

    weights = [gathered(fetched[0], span)]
    across = jnp.exp(-pole_rate * rows)
    across2 = jnp.exp(-pole_rate * (2.0 * rows))
    across4 = jnp.exp(-pole_rate * (4.0 * rows))
    theirs = other_core(span)
    chip = jnp.where(core == 0, across * span + theirs, across * theirs + span)
    behind = from_chip_behind(chip, 1) + across2 * from_chip_behind(chip, 2) + across4 * from_chip_behind(chip, 3)
    incoming = jnp.where(core == 0, behind, across * behind + theirs)

    mixed = []
    state, start = excl, 0
    for i, tc in enumerate(tcs):
        sent, state = conv_chunk(
            pos, q3, k3, v3, pole_rate, pole_residue, skip_gain, state, incoming if i == 0 else None,
            start // tc, tc, i == len(tcs) - 1)
        if i + 1 < len(fetched):
            weights.append(gathered(fetched[i + 1], sent[0]))
        mixed.append([sent[0]] + [over_y(piece, step) for piece, step in zip(sent[1:], STEPS)])
        start += tc

    def reduced(part):
        arrived = [part[0]] + [over_z(part[step % NZ], step) for step in STEPS]
        return sum(p.astype(jnp.float32) for p in arrived).astype(jnp.bfloat16)

    pieces, places = [], []
    for k, (row_set, col_set) in enumerate(TILES):
        split = k in OFFLOADED
        weight = out_weight
        if k:
            weight = lax.optimization_barrier((weight, part[0]))[0]
        part = tile(
            pos, weight, [mixed[i] for i in row_set], [weights[g] for g in col_set],
            tuple(cols[g] for g in col_set), tuple(offsets[g] for g in col_set), half_cols, split)
        if split:
            flat = part[0].reshape(-1, part[0].shape[-1])
            groups = [[y * NZ + z for z in range(NZ)] for y in range(NY)]
            flat = lax.psum_scatter(flat, "chan", scatter_dimension=0, axis_index_groups=groups, tiled=True)
            send, keep = flat.reshape(part[0].shape[1:])
        else:
            send, keep = reduced(part)
        row = sum(tcs[:row_set[0]])
        size = sum(tcs[i] for i in row_set)
        col = offsets[col_set[0]]
        n = sum(cols[g] for g in col_set)
        pieces += [keep, with_partner(send)]
        places += [(0, row, size, col, n), (1, row, size, col, n)]
    return place(pos, pieces, places, (per, total_cols), half_cols)


def solution(mesh):
    in_specs = (
        P("seq", "chan"),
        P("seq", "chan"),
        P("seq", "chan"),
        P(None, "chan"),
        P(None, "chan"),
        P("chan"),
        P("chan", None),
    )
    out_specs = P(("seq", "chan"), None)
    return jax.shard_map(local, mesh=mesh, in_specs=in_specs, out_specs=out_specs, check_vma=False)
```

```python
import functools

import jax
import jax.numpy as jnp
from jax import lax
from jax.experimental import pallas as pl
from jax.experimental.pallas import tpu as pltpu
from jax.sharding import PartitionSpec as P

POLES = 16
PAD = 8
LANES = 128
NX, NCORE, NY, NZ = 4, 2, 4, 4
STEPS = (1, -1, 2)
ROW_PARTS = (1, 1, 2)
COL_PARTS = (1, 1)
TILES = (((0, 1), (0,)), ((2,), (0,)), ((0, 1), (1,)), ((2,), (1,)))
OFFLOADED = ()
HBM = pl.BlockSpec(memory_space=pltpu.HBM)
SMEM = pl.BlockSpec(memory_space=pltpu.SMEM)
VMEM = pl.BlockSpec(memory_space=pltpu.VMEM)
LIMIT = pltpu.CompilerParams(vmem_limit_bytes=60 * 1024 * 1024)


def work(us):
    return pl.CostEstimate(flops=us * 1_150_000_000, bytes_accessed=0, transcendentals=0)


def over_y(value, step):
    return lax.ppermute(value, "chan", [(y * NZ + z, (y + step) % NY * NZ + z) for y in range(NY) for z in range(NZ)])


def over_z(value, step):
    return lax.ppermute(value, "chan", [(y * NZ + z, y * NZ + (z + step) % NZ) for y in range(NY) for z in range(NZ)])


def with_partner(value):
    return lax.ppermute(value, "chan", [(y * NZ + z, (y ^ 1) * NZ + z) for y in range(NY) for z in range(NZ)])


def other_core(value):
    return lax.ppermute(value, "seq", [(s, s ^ 1) for s in range(NX * NCORE)])


def from_chip_behind(value, step):
    pairs = [(x * NCORE + c, (x + step) * NCORE + c) for x in range(NX - step) for c in range(NCORE)]
    return lax.ppermute(value, "seq", pairs)


def state_kernel(k_ref, v_ref, rate_ref, excl_ref, span_ref, drive, fb, *, T, unroll):
    W = k_ref.shape[-1]
    nO = k_ref.shape[0]
    PT = T + PAD
    for o in range(nO):
        drive[pl.ds(o*PT, T), :] = k_ref[o].astype(jnp.float32) * v_ref[o].astype(jnp.float32)
    rate = rate_ref[...]
    f = jnp.exp(-rate)
    for r in range(POLES):
        fb[r] = jnp.broadcast_to(f[r:r+1], (8, W))
    oid = lax.broadcasted_iota(jnp.int32, (8, W), 0)
    prev = None
    fT = jnp.exp(-rate * T)
    finals = []
    G = nO//8
    fr = [fb[r] for r in range(POLES)]
    def body(i, s):
        s = [list(x) for x in s]
        for j in range(unroll):
            for p in range(G):
                u = drive[pl.ds(p*8*PT + i*unroll + j, 8, stride=PT), :]
                for r in range(POLES):
                    s[p][r] = fr[r]*s[p][r] + u
        return tuple(tuple(x) for x in s)
    finals = lax.fori_loop(0, T//unroll, body, tuple(tuple(jnp.zeros((8,W),jnp.float32) for _ in range(POLES)) for p in range(G)))
    spans=[]
    for r in range(POLES):
        carry = jnp.zeros((1,W),jnp.float32)
        g = fT[r:r+1]
        g2 = g*g; g4 = g2*g2; g8 = g4*g4
        pw = jnp.ones((8,W),jnp.float32)
        pw = jnp.where((oid & 1)!=0, pw*g, pw)
        pw = jnp.where((oid & 2)!=0, pw*g2, pw)
        pw = jnp.where((oid & 4)!=0, pw*g4, pw)
        for p in range(nO//8):
            s = finals[p][r]
            for d, gd in ((1,g),(2,g2),(4,g4)):
                s = s + jnp.where(oid>=d, pltpu.roll(s, d, 0), 0.0)*gd
            ex = jnp.where(oid>=1, pltpu.roll(s,1,0), 0.0) + pw*carry
            excl_ref[r, pl.ds(p*8,8), :] = ex
            carry = s[7:8] + g8*carry
        spans.append(carry)
    span_ref[...] = jnp.concatenate(spans, axis=0)

def states(k3, v3, rate, unroll=32):
    nO,T,C = k3.shape
    W=128
    return pl.pallas_call(
        functools.partial(state_kernel, T=T, unroll=unroll),
        grid=(C//W,),
        in_specs=[pl.BlockSpec((nO,T,W), lambda c:(0,0,c)), pl.BlockSpec((nO,T,W), lambda c:(0,0,c)),
                  pl.BlockSpec((POLES,W), lambda c:(0,c))],
        out_specs=[pl.BlockSpec((POLES,nO,W), lambda c:(0,0,c)), pl.BlockSpec((POLES,W), lambda c:(0,c))],
        out_shape=[jax.ShapeDtypeStruct((POLES,nO,C), jnp.float32), jax.ShapeDtypeStruct((POLES,C), jnp.float32)],
        scratch_shapes=[pltpu.VMEM((nO*(T+PAD),W), jnp.float32), pltpu.VMEM((POLES,8,W), jnp.float32)],
        compiler_params=LIMIT,
        cost_estimate=work(8),
        name="states",
    )(k3, v3, rate)


def conv_kernel(pos_ref, q_ref, k_ref, v_ref, rate_ref, res_ref, skip_ref, init_ref, *rest, unroll, per, first, last):
    rest = list(rest)
    inc_ref = rest.pop(0) if first else None
    outs = rest[:4]
    state_ref = None if last else rest[4]
    drive, y, fb, rb, mixed = rest[4 if last else 5:]
    nO, T, W = k_ref.shape
    PT = T + PAD
    for o in range(nO):
        drive[pl.ds(o * PT, T), :] = k_ref[o].astype(jnp.float32) * v_ref[o].astype(jnp.float32)
    rate = rate_ref[...]
    f = jnp.exp(-rate)
    for r in range(POLES):
        fb[r] = jnp.broadcast_to(f[r:r + 1], (8, W))
        rb[r] = jnp.broadcast_to(res_ref[r:r + 1], (8, W))
    rb[POLES] = jnp.broadcast_to(skip_ref[...], (8, W))
    fr = [fb[r] for r in range(POLES)]
    G = nO // 8

    def begin(p, r):
        s = init_ref[r, pl.ds(p * 8, 8), :]
        if first:
            owner = (lax.broadcasted_iota(jnp.int32, (8, W), 0) + p * 8).astype(jnp.float32)
            s = s + jnp.exp(-(rate[r:r + 1] * float(per)) * owner) * inc_ref[r:r + 1]
        return s

    def body(i, s):
        s = [list(x) for x in s]
        for j in range(unroll):
            t = i * unroll + j
            us = [drive[pl.ds(p * 8 * PT + t, 8, stride=PT), :] for p in range(G)]
            acc = [[rb[POLES] * us[p], None] for p in range(G)]
            for r in range(POLES):
                rr = rb[r]
                for p in range(G):
                    s[p][r] = fr[r] * s[p][r] + us[p]
                    m = rr * s[p][r]
                    acc[p][r % 2] = m if acc[p][r % 2] is None else acc[p][r % 2] + m
            for p in range(G):
                y[pl.ds(p * 8 * PT + t, 8, stride=PT), :] = acc[p][0] + acc[p][1]
        return tuple(tuple(x) for x in s)

    s = lax.fori_loop(0, T // unroll, body, tuple(tuple(begin(p, r) for r in range(POLES)) for p in range(G)))
    if not last:
        for p in range(G):
            for r in range(POLES):
                state_ref[r, pl.ds(p * 8, 8), :] = s[p][r]
    for o in range(nO):
        mixed[o] = (q_ref[o].astype(jnp.float32) * y[pl.ds(o * PT, T), :]).astype(jnp.bfloat16)
    my_y, my_z = pos_ref[0], pos_ref[1]
    for out_ref, step in zip(outs, (0,) + STEPS):
        half = lax.rem(my_y + step + NY, NY) // 2
        for zr in range(NZ):
            z = lax.rem(my_z + zr, NZ)
            for yl in range(2):
                out_ref[zr, yl] = mixed[half * 8 + yl * NZ + z]


def conv_chunk(pos, q3, k3, v3, rate, res, skip, init, inc, index, tc, last):
    nO, T, C = k3.shape
    W = LANES
    first = inc is not None
    row = pl.BlockSpec((nO, tc, W), lambda c: (0, index, c))
    par = pl.BlockSpec((POLES, W), lambda c: (0, c))
    st = pl.BlockSpec((POLES, nO, W), lambda c: (0, 0, c))
    ops = [pos, q3, k3, v3, rate, res, skip.reshape(1, -1), init]
    specs = [SMEM, row, row, row, par, par, pl.BlockSpec((1, W), lambda c: (0, c)), st]
    if first:
        ops.append(inc)
        specs.append(par)
    out = pltpu.HBM((NZ, 2, tc, C), jnp.bfloat16)
    out_shape = [out] * 4
    out_specs = [pl.BlockSpec((NZ, 2, tc, W), lambda c: (0, 0, 0, c))] * 4
    if not last:
        out_shape = out_shape + [jax.ShapeDtypeStruct((POLES, nO, C), jnp.float32)]
        out_specs = out_specs + [st]
    res = pl.pallas_call(
        functools.partial(conv_kernel, unroll=32, per=T, first=first, last=last),
        grid=(C // W,),
        in_specs=specs,
        out_specs=out_specs,
        out_shape=out_shape,
        scratch_shapes=[
            pltpu.VMEM((nO * (tc + PAD), W), jnp.float32),
            pltpu.VMEM((nO * (tc + PAD), W), jnp.float32),
            pltpu.VMEM((POLES, 8, W), jnp.float32),
            pltpu.VMEM((POLES + 1, 8, W), jnp.float32),
            pltpu.VMEM((nO, tc, W), jnp.bfloat16),
        ],
        compiler_params=LIMIT,
        cost_estimate=work(8),
        name="conv",
    )(*ops)
    return res[:4], (None if last else res[4])


def share_kernel(pos_ref, w_ref, *refs, widths, offsets, half_cols):
    n = len(widths) * len(STEPS)
    outs, sems = refs[:n], refs[n]
    copies = []
    for g, (width, offset) in enumerate(zip(widths, offsets)):
        for i, step in enumerate(STEPS):
            half = lax.rem(lax.rem(pos_ref[0] + step + NY, NY), 2)
            col = pl.multiple_of(half * half_cols + offset + pos_ref[2] * width, LANES)
            k = g * len(STEPS) + i
            copies.append(pltpu.make_async_copy(w_ref.at[:, pl.ds(col, width)], outs[k], sems.at[k]))
    for c in copies:
        c.start()
    for c in copies:
        c.wait()


def weight_shares(pos, weight, widths, offsets, half_cols):
    k = weight.shape[0]
    n = len(widths) * len(STEPS)
    out = pl.pallas_call(
        functools.partial(share_kernel, widths=widths, offsets=offsets, half_cols=half_cols),
        in_specs=[SMEM, HBM],
        out_specs=[VMEM] * n,
        out_shape=[jax.ShapeDtypeStruct((k, w), weight.dtype) for w in widths for _ in STEPS],
        scratch_shapes=[pltpu.SemaphoreType.DMA((n,))],
        compiler_params=LIMIT,
        name="weight_shares",
    )(pos, weight)
    return [out[g * len(STEPS):(g + 1) * len(STEPS)] for g in range(len(widths))]


def tile_kernel(pos_ref, w_ref, *refs, row_sizes, cols, offsets, half_cols, block, split):
    nr, nc = len(row_sizes), len(cols)
    a_refs, b_refs = refs[:4 * nr], refs[4 * nr:4 * nr + nc]
    n_out = 1 if split else NZ
    outs = refs[4 * nr + nc:4 * nr + nc + n_out]
    a_v, b_v, out_v, sem_a, sem_b, sem_w, sem_out = refs[4 * nr + nc + n_out:]
    width = w_ref.shape[0]
    total = sum(row_sizes)
    a_copies = []
    start = 0
    for i, tc in enumerate(row_sizes):
        for d in range(4):
            dst = a_v.at[:, :, pl.ds(start, tc), pl.ds(d * width, width)]
            a_copies.append(pltpu.make_async_copy(a_refs[4 * i + d], dst, sem_a.at[4 * i + d]))
        start += tc
    blocks = []
    base = 0
    n = 0
    for g, (size, offset) in enumerate(zip(cols, offsets)):
        piece = size // (NX * NCORE)
        for start in range(0, size, block):
            here = []
            col = pl.multiple_of(lax.rem(pos_ref[0], 2) * half_cols + offset + start, LANES)
            nb = (base + start) // block
            here.append(pltpu.make_async_copy(
                w_ref.at[:, pl.ds(col, block)], b_v.at[pl.ds(0, width), pl.ds(base + start, block)], sem_w.at[nb]))
            for s in range(start // piece, (start + block) // piece):
                here.append(pltpu.make_async_copy(
                    b_refs[g].at[s], b_v.at[pl.ds(width, 3 * width), pl.ds(base + s * piece, piece)], sem_b.at[n]))
                n += 1
            blocks.append(here)
        base += size

    def begin(nb):
        if nb < len(blocks):
            for c in blocks[nb]:
                c.start()

    for c in a_copies:
        c.start()
    begin(0)
    for c in a_copies:
        c.wait()
    begin(1)
    begin(2)
    out_copies = []
    a = a_v[...].reshape(NZ * 2 * total, 4 * width)
    for nb, here in enumerate(blocks):
        for c in here:
            c.wait()
        begin(nb + 3)
        at = pl.ds(nb * block, block)
        part = jnp.dot(a, b_v[:, at], preferred_element_type=jnp.float32).astype(jnp.bfloat16)
        out_v[:, :, :, at] = part.reshape(NZ, 2, total, block)
        for zr in range(NZ):
            pairs = []
            for i in range(2):
                src = out_v.at[zr, lax.rem(pos_ref[0] + 1 + i, 2), :, at]
                dst = outs[0].at[lax.rem(pos_ref[1] + zr, NZ), i, :, at] if split else outs[zr].at[i, :, at]
                pairs.append((src, dst))
            for src, dst in pairs:
                c = pltpu.make_async_copy(src, dst, sem_out.at[len(out_copies)])
                c.start()
                out_copies.append(c)
    for c in out_copies:
        c.wait()


def tile(pos, weight, a_parts, b_parts, cols, offsets, half_cols, split):
    width = weight.shape[0]
    row_sizes = tuple(a[0].shape[2] for a in a_parts)
    total, n = sum(row_sizes), sum(cols)
    block = 512
    flat = [piece for a in a_parts for piece in a]
    outs = [pltpu.HBM((NZ, 2, total, n), jnp.bfloat16)] if split else [pltpu.HBM((2, total, n), jnp.bfloat16)] * NZ
    return pl.pallas_call(
        functools.partial(tile_kernel, row_sizes=row_sizes, cols=cols, offsets=offsets, half_cols=half_cols, block=block, split=split),
        in_specs=[SMEM, HBM] + [HBM] * (len(flat) + len(b_parts)),
        out_specs=[HBM] * len(outs),
        out_shape=outs,
        scratch_shapes=[
            pltpu.VMEM((NZ, 2, total, 4 * width), jnp.bfloat16),
            pltpu.VMEM((4 * width, n), jnp.bfloat16),
            pltpu.VMEM((NZ, 2, total, n), jnp.bfloat16),
            pltpu.SemaphoreType.DMA((len(flat),)),
            pltpu.SemaphoreType.DMA((NX * NCORE * len(cols),)),
            pltpu.SemaphoreType.DMA((n // block,)),
            pltpu.SemaphoreType.DMA((n // block * 2 * NZ,)),
        ],
        compiler_params=LIMIT,
        cost_estimate=work(9),
        name="tile",
    )(pos, weight, *flat, *b_parts)


def place_kernel(pos_ref, *refs, places, half_cols):
    n = len(places)
    ins, out, sems = refs[:n], refs[n], refs[n + 1]
    copies = []
    for i, (other, row, rows, col, cols) in enumerate(places):
        at = pl.multiple_of(lax.rem(pos_ref[0] + other, 2) * half_cols + col, LANES)
        copies.append(pltpu.make_async_copy(ins[i], out.at[pl.ds(row, rows), pl.ds(at, cols)], sems.at[i]))
    for c in copies:
        c.start()
    for c in copies:
        c.wait()


def place(pos, pieces, places, shape, half_cols):
    return pl.pallas_call(
        functools.partial(place_kernel, places=tuple(places), half_cols=half_cols),
        in_specs=[SMEM] + [pl.BlockSpec(memory_space=pl.ANY)] * len(pieces),
        out_specs=VMEM,
        out_shape=jax.ShapeDtypeStruct(shape, jnp.bfloat16),
        scratch_shapes=[pltpu.SemaphoreType.DMA((len(pieces),))],
        compiler_params=pltpu.CompilerParams(vmem_limit_bytes=32 * 1024 * 1024),
        name="place",
    )(pos, *pieces)


def local(query_proj, key_proj, value_proj, pole_rate, pole_residue, skip_gain, out_weight):
    rows, width = key_proj.shape
    owners = NY * NZ
    per = rows // owners
    total_cols = out_weight.shape[1]
    half_cols = total_cols // 2
    seq, chan = lax.axis_index("seq"), lax.axis_index("chan")
    my_y, my_z, core = chan // NZ, chan % NZ, seq % NCORE
    pos = jnp.stack([my_y, my_z, seq]).astype(jnp.int32)
    unit = per // sum(ROW_PARTS)
    tcs = [unit * n for n in ROW_PARTS]
    unit = half_cols // sum(COL_PARTS)
    cols = [unit * n for n in COL_PARTS]
    offsets = [sum(cols[:g]) for g in range(len(cols))]

    shares = weight_shares(pos, out_weight, [c // (NX * NCORE) for c in cols], offsets, half_cols)
    fetched = [[over_y(piece, step) for piece, step in zip(group, STEPS)] for group in shares]

    q3, k3, v3 = [x.reshape(owners, per, width) for x in (query_proj, key_proj, value_proj)]
    k3 = lax.optimization_barrier((k3, shares[0][0]))[0]
    excl, span = states(k3, v3, pole_rate)

    def gathered(group, after):
        _, *pieces = lax.optimization_barrier((after, *group))
        return lax.all_gather(jnp.concatenate(pieces, axis=0), "seq", axis=0)


    across = jnp.exp(-pole_rate * rows)
    across2 = jnp.exp(-pole_rate * (2.0 * rows))
    across4 = jnp.exp(-pole_rate * (4.0 * rows))
    theirs = other_core(span)
    chip = jnp.where(core == 0, across * span + theirs, across * theirs + span)
    behind = from_chip_behind(chip, 1) + across2 * from_chip_behind(chip, 2) + across4 * from_chip_behind(chip, 3)
    incoming = jnp.where(core == 0, behind, across * behind + theirs)

    weights = [gathered(fetched[0], chip)]

    mixed = []
    state, start = excl, 0
    for i, tc in enumerate(tcs):
        sent, state = conv_chunk(
            pos, q3, k3, v3, pole_rate, pole_residue, skip_gain, state, incoming if i == 0 else None,
            start // tc, tc, i == len(tcs) - 1)
        if i == 1:
            weights.append(gathered(fetched[1], sent[0]))
        mixed.append([sent[0]] + [over_y(piece, step) for piece, step in zip(sent[1:], STEPS)])
        start += tc

    def reduced(part):
        arrived = [part[0]] + [over_z(part[step % NZ], step) for step in STEPS]
        return sum(p.astype(jnp.float32) for p in arrived).astype(jnp.bfloat16)

    pieces, places = [], []
    for k, (row_set, col_set) in enumerate(TILES):
        split = k in OFFLOADED
        weight = out_weight
        if k:
            weight = lax.optimization_barrier((weight, part[0]))[0]
        part = tile(
            pos, weight, [mixed[i] for i in row_set], [weights[g] for g in col_set],
            tuple(cols[g] for g in col_set), tuple(offsets[g] for g in col_set), half_cols, split)
        if split:
            flat = part[0].reshape(-1, part[0].shape[-1])
            groups = [[y * NZ + z for z in range(NZ)] for y in range(NY)]
            flat = lax.psum_scatter(flat, "chan", scatter_dimension=0, axis_index_groups=groups, tiled=True)
            send, keep = flat.reshape(part[0].shape[1:])
        else:
            send, keep = reduced(part)
        row = sum(tcs[:row_set[0]])
        size = sum(tcs[i] for i in row_set)
        col = offsets[col_set[0]]
        n = sum(cols[g] for g in col_set)
        pieces += [keep, with_partner(send)]
        places += [(0, row, size, col, n), (1, row, size, col, n)]
    return place(pos, pieces, places, (per, total_cols), half_cols)


def solution(mesh):
    in_specs = (
        P("seq", "chan"),
        P("seq", "chan"),
        P("seq", "chan"),
        P(None, "chan"),
        P(None, "chan"),
        P("chan"),
        P("chan", None),
    )
    out_specs = P(("seq", "chan"), None)
    return jax.shard_map(local, mesh=mesh, in_specs=in_specs, out_specs=out_specs, check_vma=False)
```
